32 devices in a mesh: tm: 4 (over y, core), sx: 2 (over x), sy: 4 (over z).
Axes of the slice: x: 2, y: 2, z: 4, core: 2. Of those that a mesh axis runs over, the one named last changes fastest.
Arguments:
- state_old: float32 [4, 2, 128, 2048], P('tm', None, 'sx', 'sy'), may hold values from 0 to 1
- classes: int32 [128, 2048], P('sx', 'sy'), may hold values from 0 to 7
- seeds: int32 [128, 2048], P('sx', 'sy'), may hold values 0 or 1
- material_coef: float32 [4, 8], replicated, may hold values from 0.5 to 1
- coarse_decay: float32 [4, 2, 8], replicated, may hold values from 0 to 1, as said below
Outputs:
- new_states: float32 [4, 2, 128, 2048], P('tm', None, 'sx', 'sy')
The draws below stay inside these ranges and needn't reach their ends.
Inputs may be any that keep to these rules, and one draw needn't show every extreme that they name: `coarse_decay`: each entry is a per-slice decay factor between 0 and 1.
All inputs are finite; a program needn't handle non-finite values. No bound on the sum of `seeds` on one device may be relied on, other than what follows from the above.
Results may differ from the reference program's by a relative error of at most 0.0001.
Values sent between devices are 32-bit elements; how exact they have to be, the bound alone decides.
A program may use at most 64 MiB of HBM per device.

```python
import math
import jax
import jax.numpy as jnp

SUBSTEPS = 4
CLASSES = 8
TIME_SEGMENTS = 4
NX = 128
NY = 2048


def draw_coarse_decay(key, part):
    key = jax.random.fold_in(key, 11)
    growth_rate_key, rupture_key, threshold_key = jax.random.split(key, 3)
    rates = jnp.exp(jax.random.uniform(growth_rate_key, (2, CLASSES), jnp.float32, math.log(0.02), math.log(3.0)))
    baseline_level = jnp.exp(-rates)
    rupture_event = jax.random.randint(rupture_key, (TIME_SEGMENTS, 1, 1), 0, 4) == 0
    threshold_value = jax.random.uniform(threshold_key, (TIME_SEGMENTS, 2, CLASSES), jnp.float32, 0.5, 0.8)
    coefficient_table = baseline_level[None] * jnp.where(rupture_event, threshold_value, jnp.float32(1.0))
    return coefficient_table.astype(jnp.float32)


def touch_ends(entries, stream_key, smallest, high):
    longest = entries.shape.index(max(entries.shape))
    spots = []
    for shift in (0, 1):
        where = [jax.random.randint(jax.random.fold_in(stream_key, axis), (), 0, length) for axis, length in enumerate(entries.shape)]
        where[longest] = (where[longest] + shift) % entries.shape[longest]
        spots.append(tuple(where))
    return entries.at[spots[0]].set(smallest).at[spots[1]].set(high)


def block_scale(key, dims, shards, least, high):
    def one(axis_at, shards_of):
        heights = jax.random.uniform(jax.random.fold_in(jax.random.fold_in(key, 6), axis_at), (shards_of,), jnp.float32, least / len(shards), high / len(shards))
        return jnp.repeat(jnp.exp(heights), dims[axis_at] // shards_of).reshape((-1,) + (1,) * (len(dims) - axis_at - 1))

    gain = one(*shards[0])
    for cut in shards[1:]:
        gain = gain * one(*cut)
    return gain


def setup_inputs(seed: int = 0) -> dict:
    keys = jax.random.split(jax.random.key(seed), 6)
    return {
        "state_old": jnp.clip(1.0 * jax.random.uniform(keys[0], (TIME_SEGMENTS, 2, NX, NY), jnp.float32) ** block_scale(keys[0], (TIME_SEGMENTS, 2, NX, NY), ((0, 4), (2, 2), (3, 4)), -0.2, 0.2), 0.0, 1.0),
        "classes": touch_ends(jax.random.randint(keys[1], (NX, NY), 0, CLASSES), jax.random.fold_in(keys[1], 1), 0, CLASSES - 1).astype(jnp.int32),
        "seeds": touch_ends((jax.random.randint(keys[2], (NX, NY), 0, 64) < 1).astype(jnp.int32), jax.random.fold_in(keys[2], 1), 0, 1),
        "material_coef": jnp.clip(jax.random.uniform(keys[3], (4, CLASSES), jnp.float32, 0.5, 1.0), 0.5, 1.0),
        "coarse_decay": draw_coarse_decay(jax.random.fold_in(keys[5], 71), 0),
    }


def lookup(classes, coefficient_table):
    count = coefficient_table.shape[1]
    onehot = (classes[None, :, :] == jnp.arange(count, dtype=jnp.int32)[:, None, None]).astype(jnp.float32)
    return jnp.sum(coefficient_table[:, :, None, None] * onehot[None], axis=1)


def advance(padded, coef):
    centre = padded[:, 1:-1, 1:-1]
    lap = padded[:, 2:, 1:-1] + padded[:, :-2, 1:-1] + padded[:, 1:-1, 2:] + padded[:, 1:-1, :-2] - 4.0 * centre
    damage = centre[0]
    moist = centre[1]
    moist_new = moist + 0.24 * coef[0] * lap[1] - 0.05 * coef[3] * moist
    dryness = 1.0 - moist
    damage_new = damage + 0.15 * coef[1] * lap[0] + 0.15 * (2.0 * (1.0 - damage) * coef[2] * dryness * dryness - damage)
    damage_new = jnp.maximum(damage_new, coef[4])
    return jnp.stack([damage_new, moist_new])


def fine_run(state, coef):
    for step in range(SUBSTEPS):
        state = advance(jnp.pad(state, ((0, 0), (1, 1), (1, 1))), coef)
    return state


def reference(state_old, classes, seeds, material_coef, coarse_decay):
    coef = jnp.concatenate([lookup(classes, material_coef), seeds.astype(jnp.float32)[None]], axis=0)
    outs = []
    current = state_old[0]
    for slot in range(TIME_SEGMENTS):
        fine_end = fine_run(state_old[slot], coef)
        if slot == 0:
            current = fine_end
        else:
            factor = lookup(classes, coarse_decay[slot])
            current = factor * current + (fine_end - factor * state_old[slot])
        outs.append(current)
    return jnp.stack(outs)
```

```python
import functools

import jax
import jax.numpy as jnp
from jax import lax
from jax.experimental import pallas as pl
from jax.experimental.pallas import tpu as pltpu
from jax.sharding import PartitionSpec as P

SUBSTEPS = 4
LANES = 128
ROWS = 8
TABLES = 5


def pick(bits, values):
    for bit in bits:
        values = [jnp.where(bit, values[2 * i + 1], values[2 * i]) for i in range(len(values) // 2)]
    return values[0]


def bits_of(classes):
    return [(classes & (1 << b)) != 0 for b in range(3)]


def kernel(
    sizes, state_hbm, classes_hbm, seeds_hbm, mat, decay, out_hbm,
    start, ping, pong, coef, factor, cls, sds, inbox, outbox,
    row_out, row_in, col_out, col_in, diag_in,
    load_sem, row_send, row_recv, col_send, col_recv, diag_send, diag_recv, chain_send, chain_recv, store_sem,
):
    n_t, n_x, n_y, height, width = sizes
    groups = height // ROWS
    slot, px, py = lax.axis_index("tm"), lax.axis_index("sx"), lax.axis_index("sy")
    f32 = jnp.float32

    has_x = [px > 0, px < n_x - 1]
    has_y = [py > 0, py < n_y - 1]
    to_x = [px - 1, px + 1]
    to_y = [py - 1, py + 1]
    peers = []
    for a in range(2):
        peers.append((has_x[a], {"sx": to_x[a]}))
        peers.append((has_y[a], {"sy": to_y[a]}))
        for b in range(2):
            peers.append((jnp.logical_and(has_x[a], has_y[b]), {"sx": to_x[a], "sy": to_y[b]}))
    peers.append((slot > 0, {"tm": slot - 1}))
    peers.append((slot < n_t - 1, {"tm": slot + 1}))

    loads = [
        pltpu.make_async_copy(state_hbm, start.at[:, pl.ds(0, height), pl.ds(0, width)], load_sem.at[0]),
        pltpu.make_async_copy(classes_hbm, cls, load_sem.at[1]),
        pltpu.make_async_copy(seeds_hbm, sds, load_sem.at[2]),
    ]
    for load in loads:
        load.start()

    barrier = pltpu.get_barrier_semaphore()
    total = jnp.int32(0)
    for there, where in peers:
        total = total + there.astype(jnp.int32)

        @pl.when(there)
        def _():
            pl.semaphore_signal(barrier, inc=1, device_id=where, device_id_type=pl.DeviceIdType.MESH)

    for load in loads:
        load.wait()

    lane = lax.broadcasted_iota(jnp.int32, (ROWS, LANES), 1)
    sub = lax.broadcasted_iota(jnp.int32, (ROWS, LANES), 0)
    sub_wide = lax.broadcasted_iota(jnp.int32, (ROWS, width), 0)

    def field(f, rows, cols):
        if f < 2:
            return start[f, rows, cols]
        return (cls if f == 2 else sds)[rows, cols].astype(f32)

    for side in range(2):
        rows = pl.ds(0, ROWS) if side == 0 else pl.ds(height - ROWS, ROWS)
        keep = (sub_wide < 4) if side == 0 else (sub_wide >= 4)
        for pair in range(2):
            one = field(2 * pair, rows, pl.ds(0, width))
            two = pltpu.roll(field(2 * pair + 1, rows, pl.ds(0, width)), 4, 0)
            row_out[side, pl.ds(ROWS * pair, ROWS), :] = jnp.where(keep, one, two)
    for side in range(2):
        cols = pl.ds(0, LANES) if side == 0 else pl.ds(width - LANES, LANES)
        packed = jnp.zeros((ROWS, LANES), f32)
        for g in range(groups):
            for f in range(4):
                at = 16 * g + 4 * f
                tile = field(f, pl.ds(ROWS * g, ROWS), cols)
                shift = (at if side == 0 else at + 4) % LANES
                if shift:
                    tile = pltpu.roll(tile, shift, 1)
                packed = jnp.where((lane >= at) & (lane < at + 4), tile, packed)
        col_out[side] = packed

    pl.semaphore_wait(barrier, total)

    sends = []
    for a in range(2):
        sends.append((has_x[a], has_x[1 - a], pltpu.make_async_remote_copy(
            row_out.at[a], row_in.at[1 - a], row_send.at[a], row_recv.at[1 - a],
            device_id={"sx": to_x[a]}, device_id_type=pl.DeviceIdType.MESH)))
        sends.append((has_y[a], has_y[1 - a], pltpu.make_async_remote_copy(
            col_out.at[a], col_in.at[1 - a], col_send.at[a], col_recv.at[1 - a],
            device_id={"sy": to_y[a]}, device_id_type=pl.DeviceIdType.MESH)))
        for b in range(2):
            sends.append((
                jnp.logical_and(has_x[a], has_y[b]), jnp.logical_and(has_x[1 - a], has_y[1 - b]),
                pltpu.make_async_remote_copy(
                    col_out.at[b], diag_in.at[1 - a, 1 - b], diag_send.at[a, b], diag_recv.at[1 - a, 1 - b],
                    device_id={"sx": to_x[a], "sy": to_y[b]}, device_id_type=pl.DeviceIdType.MESH)))
    for there, _, copy in sends:
        @pl.when(there)
        def _():
            copy.start()

    for a in range(2):
        @pl.when(jnp.logical_not(has_x[a]))
        def _():
            row_in[a] = jnp.zeros_like(row_in[a])

        @pl.when(jnp.logical_not(has_y[a]))
        def _():
            col_in[a] = jnp.zeros_like(col_in[a])

        for b in range(2):
            @pl.when(jnp.logical_not(jnp.logical_and(has_x[a], has_y[b])))
            def _():
                diag_in[a, b] = jnp.zeros_like(diag_in[a, b])

    c0, c1, c2, c3 = [[mat[i, c] for c in range(8)] for i in range(4)]
    tables = [
        [0.24 * c0[c] for c in range(8)],
        [1.0 - 0.96 * c0[c] - 0.05 * c3[c] for c in range(8)],
        [0.15 * c1[c] for c in range(8)],
        [0.85 - 0.6 * c1[c] for c in range(8)],
        [0.3 * c2[c] for c in range(8)],
    ]
    factors = [[decay[slot, f, c] for c in range(8)] for f in range(2)]

    for g in range(groups):
        rows = pl.ds(ROWS * g, ROWS)
        bits = bits_of(cls[rows, :])
        for t in range(TABLES):
            coef[t, rows, pl.ds(0, width)] = pick(bits, tables[t])
        coef[TABLES, rows, pl.ds(0, width)] = sds[rows, :].astype(f32)
        for f in range(2):
            factor[f, rows, :] = pick(bits, factors[f])

    for _, here, copy in sends:
        @pl.when(here)
        def _():
            copy.wait_recv()

    def fill(rows, cols, values, mask):
        start[0, rows, cols] = values[0]
        start[1, rows, cols] = values[1]
        bits = bits_of(values[2].astype(jnp.int32))
        for t in range(TABLES):
            coef[t, rows, cols] = pick(bits, tables[t]) * mask
        coef[TABLES, rows, cols] = values[3] * mask

    as_f = lambda flag: flag.astype(jnp.int32).astype(f32)
    flag_x = [as_f(v) for v in has_x]
    flag_y = [as_f(v) for v in has_y]

    low = sub_wide < 4
    values = []
    for pair in range(2):
        below = row_in[1, pl.ds(ROWS * pair, ROWS), :]
        above = row_in[0, pl.ds(ROWS * pair, ROWS), :]
        values.append(jnp.where(low, below, above))
        values.append(pltpu.roll(jnp.where(low, above, below), 4, 0))
    fill(pl.ds(height, ROWS), pl.ds(0, width), values, jnp.where(low, flag_x[1], flag_x[0]))

    first, last = lane < 4, lane >= LANES - 4
    col_mask = jnp.where(first, flag_y[1], jnp.where(last, flag_y[0], 0.0))

    def unpack(right, left, g, f):
        at = 16 * g + 4 * f
        r = pltpu.roll(right, (LANES - at) % LANES, 1) if at else right
        l = pltpu.roll(left, (LANES - 4 - at) % LANES, 1) if at != LANES - 4 else left
        return jnp.where(first, r, jnp.where(last, l, 0.0))

    right, left = col_in[1], col_in[0]
    for g in range(groups):
        fill(
            pl.ds(ROWS * g, ROWS), pl.ds(width, LANES),
            [unpack(right, left, g, f) for f in range(4)], col_mask,
        )
    low = sub < 4
    values = []
    for f in range(4):
        below = unpack(diag_in[1, 1], diag_in[1, 0], 0, f)
        above = unpack(diag_in[0, 1], diag_in[0, 0], groups - 1, f)
        values.append(jnp.where(low, below, above))
    fill(
        pl.ds(height, ROWS), pl.ds(width, LANES), values,
        col_mask * jnp.where(low, flag_x[1], flag_x[0]),
    )

    full = width + LANES
    sub_full = lax.broadcasted_iota(jnp.int32, (ROWS, full), 0)
    count = groups + 1

    def around(x, before, after):
        up = jnp.where(sub_full == 0, pltpu.roll(before, 1, 0), pltpu.roll(x, 1, 0))
        down = jnp.where(sub_full == ROWS - 1, pltpu.roll(after, ROWS - 1, 0), pltpu.roll(x, ROWS - 1, 0))
        return up + down + pltpu.roll(x, 1, 1) + pltpu.roll(x, full - 1, 1)

    def advance(src, g):
        rows = pl.ds(ROWS * g, ROWS)
        near = [pl.ds(ROWS * ((g - 1) % count), ROWS), pl.ds(ROWS * ((g + 1) % count), ROWS)]
        d, m = src[0, rows, :], src[1, rows, :]
        d_sum = around(d, src[0, near[0], :], src[0, near[1], :])
        m_sum = around(m, src[1, near[0], :], src[1, near[1], :])
        t = [coef[i, rows, :] for i in range(TABLES + 1)]
        dry = 1.0 - m
        m_new = t[1] * m + t[0] * m_sum
        d_new = t[3] * d + t[2] * d_sum + t[4] * (1.0 - d) * (dry * dry)
        return jnp.maximum(d_new, t[5]), m_new

    for src, dst in ((start, ping), (ping, pong), (pong, ping)):
        for g in range(count):
            new = advance(src, g)
            for f in range(2):
                dst[f, pl.ds(ROWS * g, ROWS), :] = new[f]

    for g in range(groups):
        rows = pl.ds(ROWS * g, ROWS)
        new = [v[:, :width] for v in advance(ping, g)]

        pass_on = pltpu.make_async_remote_copy(
            outbox.at[:, rows, :], inbox.at[:, rows, :], chain_send.at[g], chain_recv.at[g],
            device_id={"tm": slot + 1}, device_id_type=pl.DeviceIdType.MESH)

        @pl.when(slot == 0)
        def _():
            for f in range(2):
                outbox[f, rows, :] = new[f]
            pass_on.start()

        @pl.when(slot > 0)
        def _():
            for f in range(2):
                outbox[f, rows, :] = new[f] - factor[f, rows, :] * start[f, rows, pl.ds(0, width)]

    for g in range(groups):
        rows = pl.ds(ROWS * g, ROWS)
        pass_on = pltpu.make_async_remote_copy(
            outbox.at[:, rows, :], inbox.at[:, rows, :], chain_send.at[g], chain_recv.at[g],
            device_id={"tm": slot + 1}, device_id_type=pl.DeviceIdType.MESH)

        @pl.when(slot > 0)
        def _():
            pass_on.wait_recv()
            for f in range(2):
                outbox[f, rows, :] = outbox[f, rows, :] + factor[f, rows, :] * inbox[f, rows, :]

            @pl.when(slot < n_t - 1)
            def _():
                pass_on.start()

        pltpu.make_async_copy(outbox.at[:, rows, :], out_hbm.at[:, rows, :], store_sem.at[g]).start()

    for there, _, copy in sends:
        @pl.when(there)
        def _():
            copy.wait_send()
    for g in range(groups):
        rows = pl.ds(ROWS * g, ROWS)

        @pl.when(slot < n_t - 1)
        def _():
            pltpu.make_async_remote_copy(
                outbox.at[:, rows, :], inbox.at[:, rows, :], chain_send.at[g], chain_recv.at[g],
                device_id={"tm": slot + 1}, device_id_type=pl.DeviceIdType.MESH).wait_send()

        pltpu.make_async_copy(outbox.at[:, rows, :], out_hbm.at[:, rows, :], store_sem.at[g]).wait()


def solution(mesh):
    n_t, n_x, n_y = mesh.shape["tm"], mesh.shape["sx"], mesh.shape["sy"]

    def body(state_old, classes, seeds, material_coef, coarse_decay):
        _, fields, height, width = state_old.shape
        groups = height // ROWS
        f32, dma = jnp.float32, pltpu.SemaphoreType.DMA
        big = (fields, height + ROWS, width + LANES)
        hbm = pl.BlockSpec(memory_space=pl.ANY)
        smem = pl.BlockSpec(memory_space=pltpu.SMEM)
        out = pl.pallas_call(
            functools.partial(kernel, (n_t, n_x, n_y, height, width)),
            out_shape=jax.ShapeDtypeStruct((fields, height, width), f32),
            in_specs=[hbm, hbm, hbm, smem, smem],
            out_specs=hbm,
            scratch_shapes=[
                pltpu.VMEM(big, f32),
                pltpu.VMEM(big, f32),
                pltpu.VMEM(big, f32),
                pltpu.VMEM((TABLES + 1,) + big[1:], f32),
                pltpu.VMEM((fields, height, width), f32),
                pltpu.VMEM((height, width), jnp.int32),
                pltpu.VMEM((height, width), jnp.int32),
                pltpu.VMEM((fields, height, width), f32),
                pltpu.VMEM((fields, height, width), f32),
                pltpu.VMEM((2, 2 * ROWS, width), f32),
                pltpu.VMEM((2, 2 * ROWS, width), f32),
                pltpu.VMEM((2, ROWS, LANES), f32),
                pltpu.VMEM((2, ROWS, LANES), f32),
                pltpu.VMEM((2, 2, ROWS, LANES), f32),
                dma((3,)), dma((2,)), dma((2,)), dma((2,)), dma((2,)),
                dma((2, 2)), dma((2, 2)), dma((groups,)), dma((groups,)), dma((groups,)),
            ],
            compiler_params=pltpu.CompilerParams(
                collective_id=0, has_side_effects=True, vmem_limit_bytes=24 * 1024 * 1024
            ),
        )(state_old[0], classes, seeds, material_coef, coarse_decay)
        return out[None]

    return jax.shard_map(
        body,
        mesh=mesh,
        in_specs=(P("tm", None, "sx", "sy"), P("sx", "sy"), P("sx", "sy"), P(), P()),
        out_specs=P("tm", None, "sx", "sy"),
        check_vma=False,
    )
```

```python
import functools

import jax
import jax.numpy as jnp
from jax import lax
from jax.experimental import pallas as pl
from jax.experimental.pallas import tpu as pltpu
from jax.sharding import PartitionSpec as P

SUBSTEPS = 4
LANES = 128
ROWS = 8
TABLES = 5


def pick(bits, values):
    for bit in bits:
        values = [jnp.where(bit, values[2 * i + 1], values[2 * i]) for i in range(len(values) // 2)]
    return values[0]


def bits_of(classes):
    return [(classes & (1 << b)) != 0 for b in range(3)]


def kernel(
    sizes, state_hbm, classes_hbm, seeds_hbm, mat_hbm, decay_hbm, out_hbm,
    mat, decay, start, ping, pong, coef, factor, cls, sds, inbox, outbox,
    row_out, row_in, col_out, col_in, diag_in,
    load_sem, row_send, row_recv, col_send, col_recv, diag_send, diag_recv, chain_send, chain_recv, store_sem,
):
    n_t, n_x, n_y, height, width = sizes
    groups = height // ROWS
    slot, px, py = lax.axis_index("tm"), lax.axis_index("sx"), lax.axis_index("sy")
    f32 = jnp.float32

    has_x = [px > 0, px < n_x - 1]
    has_y = [py > 0, py < n_y - 1]
    to_x = [px - 1, px + 1]
    to_y = [py - 1, py + 1]
    peers = []
    for a in range(2):
        peers.append((has_x[a], {"sx": to_x[a]}))
        peers.append((has_y[a], {"sy": to_y[a]}))
        for b in range(2):
            peers.append((jnp.logical_and(has_x[a], has_y[b]), {"sx": to_x[a], "sy": to_y[b]}))
    peers.append((slot > 0, {"tm": slot - 1}))
    peers.append((slot < n_t - 1, {"tm": slot + 1}))

    loads = [
        pltpu.make_async_copy(state_hbm, start.at[:, pl.ds(0, height), pl.ds(0, width)], load_sem.at[0]),
        pltpu.make_async_copy(classes_hbm, cls, load_sem.at[1]),
        pltpu.make_async_copy(seeds_hbm, sds, load_sem.at[2]),
        pltpu.make_async_copy(mat_hbm, mat, load_sem.at[3]),
        pltpu.make_async_copy(decay_hbm, decay, load_sem.at[4]),
    ]
    for load in loads:
        load.start()

    barrier = pltpu.get_barrier_semaphore()
    total = jnp.int32(0)
    for there, where in peers:
        total = total + there.astype(jnp.int32)

        @pl.when(there)
        def _():
            pl.semaphore_signal(barrier, inc=1, device_id=where, device_id_type=pl.DeviceIdType.MESH)

    for load in loads:
        load.wait()

    lane = lax.broadcasted_iota(jnp.int32, (ROWS, LANES), 1)
    sub = lax.broadcasted_iota(jnp.int32, (ROWS, LANES), 0)
    sub_wide = lax.broadcasted_iota(jnp.int32, (ROWS, width), 0)

    def field(f, rows, cols):
        if f < 2:
            return start[f, rows, cols]
        return (cls if f == 2 else sds)[rows, cols].astype(f32)

    for side in range(2):
        rows = pl.ds(0, ROWS) if side == 0 else pl.ds(height - ROWS, ROWS)
        keep = (sub_wide < 4) if side == 0 else (sub_wide >= 4)
        for pair in range(2):
            one = field(2 * pair, rows, pl.ds(0, width))
            two = pltpu.roll(field(2 * pair + 1, rows, pl.ds(0, width)), 4, 0)
            row_out[side, pl.ds(ROWS * pair, ROWS), :] = jnp.where(keep, one, two)
    for side in range(2):
        cols = pl.ds(0, LANES) if side == 0 else pl.ds(width - LANES, LANES)
        packed = jnp.zeros((ROWS, LANES), f32)
        for g in range(groups):
            for f in range(4):
                at = 16 * g + 4 * f
                tile = field(f, pl.ds(ROWS * g, ROWS), cols)
                shift = (at if side == 0 else at + 4) % LANES
                if shift:
                    tile = pltpu.roll(tile, shift, 1)
                packed = jnp.where((lane >= at) & (lane < at + 4), tile, packed)
        col_out[side] = packed

    pl.semaphore_wait(barrier, total)

    sends = []
    for a in range(2):
        sends.append((has_x[a], has_x[1 - a], pltpu.make_async_remote_copy(
            row_out.at[a], row_in.at[1 - a], row_send.at[a], row_recv.at[1 - a],
            device_id={"sx": to_x[a]}, device_id_type=pl.DeviceIdType.MESH)))
        sends.append((has_y[a], has_y[1 - a], pltpu.make_async_remote_copy(
            col_out.at[a], col_in.at[1 - a], col_send.at[a], col_recv.at[1 - a],
            device_id={"sy": to_y[a]}, device_id_type=pl.DeviceIdType.MESH)))
        for b in range(2):
            sends.append((
                jnp.logical_and(has_x[a], has_y[b]), jnp.logical_and(has_x[1 - a], has_y[1 - b]),
                pltpu.make_async_remote_copy(
                    col_out.at[b], diag_in.at[1 - a, 1 - b], diag_send.at[a, b], diag_recv.at[1 - a, 1 - b],
                    device_id={"sx": to_x[a], "sy": to_y[b]}, device_id_type=pl.DeviceIdType.MESH)))
    for there, _, copy in sends:
        @pl.when(there)
        def _():
            copy.start()

    for a in range(2):
        @pl.when(jnp.logical_not(has_x[a]))
        def _():
            row_in[a] = jnp.zeros_like(row_in[a])

        @pl.when(jnp.logical_not(has_y[a]))
        def _():
            col_in[a] = jnp.zeros_like(col_in[a])

        for b in range(2):
            @pl.when(jnp.logical_not(jnp.logical_and(has_x[a], has_y[b])))
            def _():
                diag_in[a, b] = jnp.zeros_like(diag_in[a, b])

    c0, c1, c2, c3 = [[mat[i, c] for c in range(8)] for i in range(4)]
    tables = [
        [0.24 * c0[c] for c in range(8)],
        [1.0 - 0.96 * c0[c] - 0.05 * c3[c] for c in range(8)],
        [0.15 * c1[c] for c in range(8)],
        [0.85 - 0.6 * c1[c] for c in range(8)],
        [0.3 * c2[c] for c in range(8)],
    ]
    factors = [[decay[slot, f, c] for c in range(8)] for f in range(2)]

    for g in range(groups):
        rows = pl.ds(ROWS * g, ROWS)
        bits = bits_of(cls[rows, :])
        for t in range(TABLES):
            coef[t, rows, pl.ds(0, width)] = pick(bits, tables[t])
        coef[TABLES, rows, pl.ds(0, width)] = sds[rows, :].astype(f32)
        for f in range(2):
            factor[f, rows, :] = pick(bits, factors[f])

    for _, here, copy in sends:
        @pl.when(here)
        def _():
            copy.wait_recv()

    def fill(rows, cols, values, mask):
        start[0, rows, cols] = values[0]
        start[1, rows, cols] = values[1]
        bits = bits_of(values[2].astype(jnp.int32))
        for t in range(TABLES):
            coef[t, rows, cols] = pick(bits, tables[t]) * mask
        coef[TABLES, rows, cols] = values[3] * mask

    as_f = lambda flag: flag.astype(jnp.int32).astype(f32)
    flag_x = [as_f(v) for v in has_x]
    flag_y = [as_f(v) for v in has_y]

    low = sub_wide < 4
    values = []
    for pair in range(2):
        below = row_in[1, pl.ds(ROWS * pair, ROWS), :]
        above = row_in[0, pl.ds(ROWS * pair, ROWS), :]
        values.append(jnp.where(low, below, above))
        values.append(pltpu.roll(jnp.where(low, above, below), 4, 0))
    fill(pl.ds(height, ROWS), pl.ds(0, width), values, jnp.where(low, flag_x[1], flag_x[0]))

    first, last = lane < 4, lane >= LANES - 4
    col_mask = jnp.where(first, flag_y[1], jnp.where(last, flag_y[0], 0.0))

    def unpack(right, left, g, f):
        at = 16 * g + 4 * f
        r = pltpu.roll(right, (LANES - at) % LANES, 1) if at else right
        l = pltpu.roll(left, (LANES - 4 - at) % LANES, 1) if at != LANES - 4 else left
        return jnp.where(first, r, jnp.where(last, l, 0.0))

    right, left = col_in[1], col_in[0]
    for g in range(groups):
        fill(
            pl.ds(ROWS * g, ROWS), pl.ds(width, LANES),
            [unpack(right, left, g, f) for f in range(4)], col_mask,
        )
    low = sub < 4
    values = []
    for f in range(4):
        below = unpack(diag_in[1, 1], diag_in[1, 0], 0, f)
        above = unpack(diag_in[0, 1], diag_in[0, 0], groups - 1, f)
        values.append(jnp.where(low, below, above))
    fill(
        pl.ds(height, ROWS), pl.ds(width, LANES), values,
        col_mask * jnp.where(low, flag_x[1], flag_x[0]),
    )

    full = width + LANES
    sub_full = lax.broadcasted_iota(jnp.int32, (ROWS, full), 0)
    count = groups + 1

    def around(x, before, after):
        up = jnp.where(sub_full == 0, pltpu.roll(before, 1, 0), pltpu.roll(x, 1, 0))
        down = jnp.where(sub_full == ROWS - 1, pltpu.roll(after, ROWS - 1, 0), pltpu.roll(x, ROWS - 1, 0))
        return up + down + pltpu.roll(x, 1, 1) + pltpu.roll(x, full - 1, 1)

    def advance(src, g):
        rows = pl.ds(ROWS * g, ROWS)
        near = [pl.ds(ROWS * ((g - 1) % count), ROWS), pl.ds(ROWS * ((g + 1) % count), ROWS)]
        d, m = src[0, rows, :], src[1, rows, :]
        d_sum = around(d, src[0, near[0], :], src[0, near[1], :])
        m_sum = around(m, src[1, near[0], :], src[1, near[1], :])
        t = [coef[i, rows, :] for i in range(TABLES + 1)]
        dry = 1.0 - m
        m_new = t[1] * m + t[0] * m_sum
        d_new = t[3] * d + t[2] * d_sum + t[4] * (1.0 - d) * (dry * dry)
        return jnp.maximum(d_new, t[5]), m_new

    for src, dst in ((start, ping), (ping, pong), (pong, ping)):
        for g in range(count):
            new = advance(src, g)
            for f in range(2):
                dst[f, pl.ds(ROWS * g, ROWS), :] = new[f]

    for g in range(groups):
        rows = pl.ds(ROWS * g, ROWS)
        new = [v[:, :width] for v in advance(ping, g)]

        pass_on = pltpu.make_async_remote_copy(
            outbox.at[:, rows, :], inbox.at[:, rows, :], chain_send.at[g], chain_recv.at[g],
            device_id={"tm": slot + 1}, device_id_type=pl.DeviceIdType.MESH)

        @pl.when(slot == 0)
        def _():
            for f in range(2):
                outbox[f, rows, :] = new[f]
            pass_on.start()

        @pl.when(slot > 0)
        def _():
            for f in range(2):
                outbox[f, rows, :] = new[f] - factor[f, rows, :] * start[f, rows, pl.ds(0, width)]

    for g in range(groups):
        rows = pl.ds(ROWS * g, ROWS)
        pass_on = pltpu.make_async_remote_copy(
            outbox.at[:, rows, :], inbox.at[:, rows, :], chain_send.at[g], chain_recv.at[g],
            device_id={"tm": slot + 1}, device_id_type=pl.DeviceIdType.MESH)

        @pl.when(slot > 0)
        def _():
            pass_on.wait_recv()
            for f in range(2):
                outbox[f, rows, :] = outbox[f, rows, :] + factor[f, rows, :] * inbox[f, rows, :]

            @pl.when(slot < n_t - 1)
            def _():
                pass_on.start()

        pltpu.make_async_copy(outbox.at[:, rows, :], out_hbm.at[:, rows, :], store_sem.at[g]).start()

    for there, _, copy in sends:
        @pl.when(there)
        def _():
            copy.wait_send()
    for g in range(groups):
        rows = pl.ds(ROWS * g, ROWS)

        @pl.when(slot < n_t - 1)
        def _():
            pltpu.make_async_remote_copy(
                outbox.at[:, rows, :], inbox.at[:, rows, :], chain_send.at[g], chain_recv.at[g],
                device_id={"tm": slot + 1}, device_id_type=pl.DeviceIdType.MESH).wait_send()

        pltpu.make_async_copy(outbox.at[:, rows, :], out_hbm.at[:, rows, :], store_sem.at[g]).wait()


def solution(mesh):
    n_t, n_x, n_y = mesh.shape["tm"], mesh.shape["sx"], mesh.shape["sy"]

    def body(state_old, classes, seeds, material_coef, coarse_decay):
        _, fields, height, width = state_old.shape
        groups = height // ROWS
        f32, dma = jnp.float32, pltpu.SemaphoreType.DMA
        big = (fields, height + ROWS, width + LANES)
        hbm = pl.BlockSpec(memory_space=pltpu.HBM)
        out = pl.pallas_call(
            functools.partial(kernel, (n_t, n_x, n_y, height, width)),
            out_shape=jax.ShapeDtypeStruct((fields, height, width), f32),
            in_specs=[hbm] * 5,
            out_specs=hbm,
            scratch_shapes=[
                pltpu.SMEM(material_coef.shape, f32),
                pltpu.SMEM(coarse_decay.shape, f32),
                pltpu.VMEM(big, f32),
                pltpu.VMEM(big, f32),
                pltpu.VMEM(big, f32),
                pltpu.VMEM((TABLES + 1,) + big[1:], f32),
                pltpu.VMEM((fields, height, width), f32),
                pltpu.VMEM((height, width), jnp.int32),
                pltpu.VMEM((height, width), jnp.int32),
                pltpu.VMEM((fields, height, width), f32),
                pltpu.VMEM((fields, height, width), f32),
                pltpu.VMEM((2, 2 * ROWS, width), f32),
                pltpu.VMEM((2, 2 * ROWS, width), f32),
                pltpu.VMEM((2, ROWS, LANES), f32),
                pltpu.VMEM((2, ROWS, LANES), f32),
                pltpu.VMEM((2, 2, ROWS, LANES), f32),
                dma((5,)), dma((2,)), dma((2,)), dma((2,)), dma((2,)),
                dma((2, 2)), dma((2, 2)), dma((groups,)), dma((groups,)), dma((groups,)),
            ],
            compiler_params=pltpu.CompilerParams(
                collective_id=0, has_side_effects=True, vmem_limit_bytes=61 * 1024 * 1024
            ),
        )(state_old[0], classes, seeds, material_coef, coarse_decay)
        return out[None]

    return jax.shard_map(
        body,
        mesh=mesh,
        in_specs=(P("tm", None, "sx", "sy"), P("sx", "sy"), P("sx", "sy"), P(), P()),
        out_specs=P("tm", None, "sx", "sy"),
        check_vma=False,
    )
```

```python
import functools

import jax
import jax.numpy as jnp
from jax import lax
from jax.experimental import pallas as pl
from jax.experimental.pallas import tpu as pltpu
from jax.sharding import PartitionSpec as P

SUBSTEPS = 4
LANES = 128
ROWS = 8
TABLES = 5


def pick(bits, values):
    for bit in bits:
        values = [jnp.where(bit, values[2 * i + 1], values[2 * i]) for i in range(len(values) // 2)]
    return values[0]


def bits_of(classes):
    return [(classes & (1 << b)) != 0 for b in range(3)]


def kernel(
    sizes, state_hbm, classes_hbm, seeds_hbm, mat_hbm, decay_hbm, outbox,
    mat, decay, start, ping, pong, coef, factor, cls, sds, inbox,
    row_out, row_in, col_out, col_in, diag_in,
    load_sem, row_send, row_recv, col_send, col_recv, diag_send, diag_recv, chain_send, chain_recv,
):
    n_t, n_x, n_y, height, width = sizes
    groups = height // ROWS
    slot, px, py = lax.axis_index("tm"), lax.axis_index("sx"), lax.axis_index("sy")
    f32 = jnp.float32

    has_x = [px > 0, px < n_x - 1]
    has_y = [py > 0, py < n_y - 1]
    to_x = [px - 1, px + 1]
    to_y = [py - 1, py + 1]
    peers = []
    for a in range(2):
        peers.append((has_x[a], {"sx": to_x[a]}))
        peers.append((has_y[a], {"sy": to_y[a]}))
        for b in range(2):
            peers.append((jnp.logical_and(has_x[a], has_y[b]), {"sx": to_x[a], "sy": to_y[b]}))
    peers.append((slot > 0, {"tm": slot - 1}))
    peers.append((slot < n_t - 1, {"tm": slot + 1}))

    loads = [
        pltpu.make_async_copy(state_hbm, start.at[:, pl.ds(0, height), pl.ds(0, width)], load_sem.at[0]),
        pltpu.make_async_copy(classes_hbm, cls, load_sem.at[1]),
        pltpu.make_async_copy(seeds_hbm, sds, load_sem.at[2]),
        pltpu.make_async_copy(mat_hbm, mat, load_sem.at[3]),
        pltpu.make_async_copy(decay_hbm, decay, load_sem.at[4]),
    ]
    for load in loads:
        load.start()

    barrier = pltpu.get_barrier_semaphore()
    total = jnp.int32(0)
    for there, where in peers:
        total = total + there.astype(jnp.int32)

        @pl.when(there)
        def _():
            pl.semaphore_signal(barrier, inc=1, device_id=where, device_id_type=pl.DeviceIdType.MESH)

    for load in loads:
        load.wait()

    lane = lax.broadcasted_iota(jnp.int32, (ROWS, LANES), 1)
    sub = lax.broadcasted_iota(jnp.int32, (ROWS, LANES), 0)
    sub_wide = lax.broadcasted_iota(jnp.int32, (ROWS, width), 0)

    def field(f, rows, cols):
        if f < 2:
            return start[f, rows, cols]
        return (cls if f == 2 else sds)[rows, cols].astype(f32)

    for side in range(2):
        rows = pl.ds(0, ROWS) if side == 0 else pl.ds(height - ROWS, ROWS)
        keep = (sub_wide < 4) if side == 0 else (sub_wide >= 4)
        for pair in range(2):
            one = field(2 * pair, rows, pl.ds(0, width))
            two = pltpu.roll(field(2 * pair + 1, rows, pl.ds(0, width)), 4, 0)
            row_out[side, pl.ds(ROWS * pair, ROWS), :] = jnp.where(keep, one, two)
    for side in range(2):
        cols = pl.ds(0, LANES) if side == 0 else pl.ds(width - LANES, LANES)
        packed = jnp.zeros((ROWS, LANES), f32)
        for g in range(groups):
            for f in range(4):
                at = 16 * g + 4 * f
                tile = field(f, pl.ds(ROWS * g, ROWS), cols)
                shift = (at if side == 0 else at + 4) % LANES
                if shift:
                    tile = pltpu.roll(tile, shift, 1)
                packed = jnp.where((lane >= at) & (lane < at + 4), tile, packed)
        col_out[side] = packed

    pl.semaphore_wait(barrier, total)

    sends = []
    for a in range(2):
        sends.append((has_x[a], has_x[1 - a], pltpu.make_async_remote_copy(
            row_out.at[a], row_in.at[1 - a], row_send.at[a], row_recv.at[1 - a],
            device_id={"sx": to_x[a]}, device_id_type=pl.DeviceIdType.MESH)))
        sends.append((has_y[a], has_y[1 - a], pltpu.make_async_remote_copy(
            col_out.at[a], col_in.at[1 - a], col_send.at[a], col_recv.at[1 - a],
            device_id={"sy": to_y[a]}, device_id_type=pl.DeviceIdType.MESH)))
        for b in range(2):
            sends.append((
                jnp.logical_and(has_x[a], has_y[b]), jnp.logical_and(has_x[1 - a], has_y[1 - b]),
                pltpu.make_async_remote_copy(
                    col_out.at[b], diag_in.at[1 - a, 1 - b], diag_send.at[a, b], diag_recv.at[1 - a, 1 - b],
                    device_id={"sx": to_x[a], "sy": to_y[b]}, device_id_type=pl.DeviceIdType.MESH)))
    for there, _, copy in sends:
        @pl.when(there)
        def _():
            copy.start()

    for a in range(2):
        @pl.when(jnp.logical_not(has_x[a]))
        def _():
            row_in[a] = jnp.zeros_like(row_in[a])

        @pl.when(jnp.logical_not(has_y[a]))
        def _():
            col_in[a] = jnp.zeros_like(col_in[a])

        for b in range(2):
            @pl.when(jnp.logical_not(jnp.logical_and(has_x[a], has_y[b])))
            def _():
                diag_in[a, b] = jnp.zeros_like(diag_in[a, b])

    c0, c1, c2, c3 = [[mat[i, c] for c in range(8)] for i in range(4)]
    tables = [
        [0.24 * c0[c] for c in range(8)],
        [1.0 - 0.96 * c0[c] - 0.05 * c3[c] for c in range(8)],
        [0.15 * c1[c] for c in range(8)],
        [0.85 - 0.6 * c1[c] for c in range(8)],
        [0.3 * c2[c] for c in range(8)],
    ]
    factors = [[decay[slot, f, c] for c in range(8)] for f in range(2)]

    for g in range(groups):
        rows = pl.ds(ROWS * g, ROWS)
        bits = bits_of(cls[rows, :])
        for t in range(TABLES):
            coef[t, rows, pl.ds(0, width)] = pick(bits, tables[t])
        coef[TABLES, rows, pl.ds(0, width)] = sds[rows, :].astype(f32)
        for f in range(2):
            factor[f, rows, :] = pick(bits, factors[f])

    for _, here, copy in sends:
        @pl.when(here)
        def _():
            copy.wait_recv()

    def fill(rows, cols, values, mask):
        start[0, rows, cols] = values[0]
        start[1, rows, cols] = values[1]
        bits = bits_of(values[2].astype(jnp.int32))
        for t in range(TABLES):
            coef[t, rows, cols] = pick(bits, tables[t]) * mask
        coef[TABLES, rows, cols] = values[3] * mask

    as_f = lambda flag: flag.astype(jnp.int32).astype(f32)
    flag_x = [as_f(v) for v in has_x]
    flag_y = [as_f(v) for v in has_y]

    low = sub_wide < 4
    values = []
    for pair in range(2):
        below = row_in[1, pl.ds(ROWS * pair, ROWS), :]
        above = row_in[0, pl.ds(ROWS * pair, ROWS), :]
        values.append(jnp.where(low, below, above))
        values.append(pltpu.roll(jnp.where(low, above, below), 4, 0))
    fill(pl.ds(height, ROWS), pl.ds(0, width), values, jnp.where(low, flag_x[1], flag_x[0]))

    first, last = lane < 4, lane >= LANES - 4
    col_mask = jnp.where(first, flag_y[1], jnp.where(last, flag_y[0], 0.0))

    def unpack(right, left, g, f):
        at = 16 * g + 4 * f
        r = pltpu.roll(right, (LANES - at) % LANES, 1) if at else right
        l = pltpu.roll(left, (LANES - 4 - at) % LANES, 1) if at != LANES - 4 else left
        return jnp.where(first, r, jnp.where(last, l, 0.0))

    right, left = col_in[1], col_in[0]
    for g in range(groups):
        fill(
            pl.ds(ROWS * g, ROWS), pl.ds(width, LANES),
            [unpack(right, left, g, f) for f in range(4)], col_mask,
        )
    low = sub < 4
    values = []
    for f in range(4):
        below = unpack(diag_in[1, 1], diag_in[1, 0], 0, f)
        above = unpack(diag_in[0, 1], diag_in[0, 0], groups - 1, f)
        values.append(jnp.where(low, below, above))
    fill(
        pl.ds(height, ROWS), pl.ds(width, LANES), values,
        col_mask * jnp.where(low, flag_x[1], flag_x[0]),
    )

    full = width + LANES
    sub_full = lax.broadcasted_iota(jnp.int32, (ROWS, full), 0)
    count = groups + 1

    def around(x, before, after):
        up = jnp.where(sub_full == 0, pltpu.roll(before, 1, 0), pltpu.roll(x, 1, 0))
        down = jnp.where(sub_full == ROWS - 1, pltpu.roll(after, ROWS - 1, 0), pltpu.roll(x, ROWS - 1, 0))
        return up + down + pltpu.roll(x, 1, 1) + pltpu.roll(x, full - 1, 1)

    def advance(src, g):
        rows = pl.ds(ROWS * g, ROWS)
        near = [pl.ds(ROWS * ((g - 1) % count), ROWS), pl.ds(ROWS * ((g + 1) % count), ROWS)]
        d, m = src[0, rows, :], src[1, rows, :]
        d_sum = around(d, src[0, near[0], :], src[0, near[1], :])
        m_sum = around(m, src[1, near[0], :], src[1, near[1], :])
        t = [coef[i, rows, :] for i in range(TABLES + 1)]
        dry = 1.0 - m
        m_new = t[1] * m + t[0] * m_sum
        d_new = t[3] * d + t[2] * d_sum + t[4] * (1.0 - d) * (dry * dry)
        return jnp.maximum(d_new, t[5]), m_new

    for src, dst in ((start, ping), (ping, pong), (pong, ping)):
        for g in range(count):
            new = advance(src, g)
            for f in range(2):
                dst[f, pl.ds(ROWS * g, ROWS), :] = new[f]

    for g in range(groups):
        rows = pl.ds(ROWS * g, ROWS)
        new = [v[:, :width] for v in advance(ping, g)]

        pass_on = pltpu.make_async_remote_copy(
            outbox.at[:, rows, :], inbox.at[:, rows, :], chain_send.at[g], chain_recv.at[g],
            device_id={"tm": slot + 1}, device_id_type=pl.DeviceIdType.MESH)

        @pl.when(slot == 0)
        def _():
            for f in range(2):
                outbox[f, rows, :] = new[f]
            pass_on.start()

        @pl.when(slot > 0)
        def _():
            for f in range(2):
                outbox[f, rows, :] = new[f] - factor[f, rows, :] * start[f, rows, pl.ds(0, width)]

    for g in range(groups):
        rows = pl.ds(ROWS * g, ROWS)
        pass_on = pltpu.make_async_remote_copy(
            outbox.at[:, rows, :], inbox.at[:, rows, :], chain_send.at[g], chain_recv.at[g],
            device_id={"tm": slot + 1}, device_id_type=pl.DeviceIdType.MESH)

        @pl.when(slot > 0)
        def _():
            pass_on.wait_recv()
            for f in range(2):
                outbox[f, rows, :] = outbox[f, rows, :] + factor[f, rows, :] * inbox[f, rows, :]

            @pl.when(slot < n_t - 1)
            def _():
                pass_on.start()

    for there, _, copy in sends:
        @pl.when(there)
        def _():
            copy.wait_send()
    for g in range(groups):
        rows = pl.ds(ROWS * g, ROWS)

        @pl.when(slot < n_t - 1)
        def _():
            pltpu.make_async_remote_copy(
                outbox.at[:, rows, :], inbox.at[:, rows, :], chain_send.at[g], chain_recv.at[g],
                device_id={"tm": slot + 1}, device_id_type=pl.DeviceIdType.MESH).wait_send()


def solution(mesh):
    n_t, n_x, n_y = mesh.shape["tm"], mesh.shape["sx"], mesh.shape["sy"]

    def body(state_old, classes, seeds, material_coef, coarse_decay):
        _, fields, height, width = state_old.shape
        groups = height // ROWS
        f32, dma = jnp.float32, pltpu.SemaphoreType.DMA
        big = (fields, height + ROWS, width + LANES)
        hbm = pl.BlockSpec(memory_space=pltpu.HBM)
        out = pl.pallas_call(
            functools.partial(kernel, (n_t, n_x, n_y, height, width)),
            out_shape=pltpu.VMEM((fields, height, width), f32),
            in_specs=[hbm] * 5,
            out_specs=pl.BlockSpec(memory_space=pltpu.VMEM),
            scratch_shapes=[
                pltpu.SMEM(material_coef.shape, f32),
                pltpu.SMEM(coarse_decay.shape, f32),
                pltpu.VMEM(big, f32),
                pltpu.VMEM(big, f32),
                pltpu.VMEM(big, f32),
                pltpu.VMEM((TABLES + 1,) + big[1:], f32),
                pltpu.VMEM((fields, height, width), f32),
                pltpu.VMEM((height, width), jnp.int32),
                pltpu.VMEM((height, width), jnp.int32),
                pltpu.VMEM((fields, height, width), f32),
                pltpu.VMEM((2, 2 * ROWS, width), f32),
                pltpu.VMEM((2, 2 * ROWS, width), f32),
                pltpu.VMEM((2, ROWS, LANES), f32),
                pltpu.VMEM((2, ROWS, LANES), f32),
                pltpu.VMEM((2, 2, ROWS, LANES), f32),
                dma((5,)), dma((2,)), dma((2,)), dma((2,)), dma((2,)),
                dma((2, 2)), dma((2, 2)), dma((groups,)), dma((groups,)),
            ],
            compiler_params=pltpu.CompilerParams(
                collective_id=0, has_side_effects=True, vmem_limit_bytes=60 * 1024 * 1024
            ),
        )(state_old[0], classes, seeds, material_coef, coarse_decay)
        return out[None]

    return jax.shard_map(
        body,
        mesh=mesh,
        in_specs=(P("tm", None, "sx", "sy"), P("sx", "sy"), P("sx", "sy"), P(), P()),
        out_specs=P("tm", None, "sx", "sy"),
        check_vma=False,
    )
```
